32 devices in a mesh: groups: 2 (over x), seq: 8 (over z, y), head: 2 (over core).
Axes of the slice: x: 2, y: 2, z: 4, core: 2. Of those that a mesh axis runs over, the one named last changes fastest.
Arguments:
- prompt_hidden: bfloat16 [192, 64, 7168], P(('groups', 'seq'), None, 'head'), parts along dimension 0, may hold values from -6 to 6
- prompt_len: int32 [192], P(('groups', 'seq')), parts along dimension 0, may hold values from 1 to 64
- prompt_dest: int32 [192], P(('groups', 'seq')), parts along dimension 0, may hold values from 0 to 95, as said below
- kv_weight: bfloat16 [7168, 576], P(('head', 'seq')), may hold values from -0.0625 to 0.0625
- kv_gain: float32 [512], replicated, may hold values from 0.1 to 1.9
- cache: bfloat16 [192, 256, 576], P(('groups', 'seq')), parts along dimension 0, may hold values from -4 to 4
- cache_len: int32 [192], P(('groups', 'seq')), parts along dimension 0, may hold values from 2 to 256
- step_hidden: bfloat16 [2, 192, 7168], P(None, ('groups', 'seq'), 'head'), parts along dimension 1, may hold values from -6 to 6
- queries: bfloat16 [2, 192, 128, 576], P(None, ('groups', 'seq'), 'head'), parts along dimension 1, may hold values from -300 to 300
Outputs:
- attended: bfloat16 [2, 192, 128, 512], P(None, ('groups', 'seq'), 'head'), parts along dimension 1
The draws below stay inside these ranges and needn't reach their ends.
There are 2 independent parts, one for each index of `groups`. The reference program is written for one: setup_inputs(seed, part) draws one part's arguments, and reference() takes and returns one part's arrays. A program takes and returns all parts, laid end to end along the dimension named above; an argument that names none is the same for every part. Nothing has to cross between parts.
Inputs may be any that keep to these rules, and one draw needn't show every extreme that they name: `prompt_dest`: A permutation of the 96 rows; row index = device index along seq times 12 plus the row within that device. The prompts of one device go to any one device either not at all or exactly 3 at a time.
All inputs are finite; a program needn't handle non-finite values.
Results may differ from the reference program's by a relative error of at most 0.0062.
Values may be sent and summed in bfloat16 or wider, within the bound.
A program may use at most 128 MiB of HBM per device.

```python
import jax
import jax.numpy as jnp
from jax import lax

D = 7168
HEADS = 128
LATENT = 512
ROPE = 64
NOPE = 128
ROWS_DEV = 12
PLEN = 64
CTX = 256
STEPS = 2
WIDTH = 576
CAP = 3
ROWS = 96
N_SEQ = 8


def anchor_keys(key):
    return jax.random.truncated_normal(key, -4.0, 4.0, (ROWS, 2, LATENT + ROPE), jnp.float32)


def draw_prompt_dest(key, part):
    key = jax.random.fold_in(key, 11)
    group_count = ROWS_DEV // CAP
    offsets = jax.random.permutation(jax.random.fold_in(key, 1), N_SEQ)[:group_count]
    source = jnp.arange(ROWS, dtype=jnp.int32) // ROWS_DEV
    within = jnp.arange(ROWS, dtype=jnp.int32) % ROWS_DEV
    target = (source + offsets[within // CAP]) % N_SEQ
    row_keys = jax.random.split(jax.random.fold_in(key, 2), N_SEQ)
    tables = jax.vmap(lambda one_key: jax.random.permutation(one_key, ROWS_DEV))(row_keys)
    return (target * ROWS_DEV + tables[target, within]).astype(jnp.int32)


def draw_cache(key, part):
    anchor = anchor_keys(key)
    key = jax.random.fold_in(key, 21)
    filler = jax.random.truncated_normal(key, -4.0, 4.0, (ROWS, CTX, LATENT + ROPE), jnp.float32)
    head_pair = anchor
    filler = filler.at[:, 0:2].set(head_pair)
    return filler.astype(jnp.bfloat16)


def draw_queries(key, part):
    key = jax.random.fold_in(key, 22)
    shape_full = (STEPS, ROWS, HEADS, LATENT + ROPE)
    base = 2.0 * jax.random.truncated_normal(key, -6.0, 6.0, shape_full, jnp.float32)
    return base.astype(jnp.bfloat16)


def touch_ends(array, own_key, least, top_value):
    longest = array.shape.index(max(array.shape))
    spots = []
    for shift in (0, 1):
        where = [jax.random.randint(jax.random.fold_in(own_key, axis), (), 0, length) for axis, length in enumerate(array.shape)]
        where[longest] = (where[longest] + shift) % array.shape[longest]
        spots.append(tuple(where))
    return array.at[spots[0]].set(least).at[spots[1]].set(top_value)


def block_levels(stream_key, extent, pieces, low, top_value):
    loudness = 1.0
    for dim, parts in pieces:
        heights = jax.random.uniform(jax.random.fold_in(jax.random.fold_in(stream_key, 6), dim), (parts,), jnp.float32, low / len(pieces), top_value / len(pieces))
        loudness = loudness * jnp.repeat(jnp.exp(heights), extent[dim] // parts).reshape((-1,) + (1,) * (len(extent) - 1 - dim))
    return loudness


def scatter_about(stream_key, extent, deviation, limit, cuts=(), kind=jnp.bfloat16):
    values = jax.random.normal(stream_key, extent, jnp.float32) * deviation
    if len(cuts) > 0:
        values = block_levels(stream_key, extent, cuts, -0.22, 0.18) * values
    return jnp.clip(values, min=-limit, max=limit).astype(kind)


def setup_inputs(seed: int = 0, part: int = 0) -> dict:
    key_of = jax.random.split(jax.random.key(seed), 10)
    part_splits = jax.random.split(jax.random.fold_in(key_of[9], part), 10)
    prompt_hidden = scatter_about(part_splits[0], (ROWS, PLEN, D), 1.0, 6.0, ((0, 8), (2, 2)))
    prompt_len = touch_ends(jax.random.randint(part_splits[1], (ROWS,), 1, PLEN + 1), jax.random.fold_in(part_splits[1], 1), 1, PLEN).astype(jnp.int32)
    prompt_dest = draw_prompt_dest(jax.random.fold_in(jax.random.fold_in(key_of[9], part), 71), part)
    kv_weight = scatter_about(key_of[3], (D, WIDTH), D ** -0.5, 0.0625, ((0, 16),))
    kv_gain = jnp.clip(1.0 + 0.18 * jax.random.normal(key_of[4], (LATENT,), jnp.float32), 0.1, 1.9)
    cache = draw_cache(jax.random.fold_in(jax.random.fold_in(key_of[9], part), 71), part)
    cache_len = touch_ends(jax.random.randint(part_splits[6], (ROWS,), 2, CTX + 1), jax.random.fold_in(part_splits[6], 1), 2, CTX).astype(jnp.int32)
    step_hidden = scatter_about(part_splits[7], (STEPS, ROWS, D), 1.0, 6.0, ((1, 8), (2, 2)))
    queries = draw_queries(jax.random.fold_in(jax.random.fold_in(key_of[9], part), 71), part)
    return {"prompt_hidden": prompt_hidden, "prompt_len": prompt_len, "prompt_dest": prompt_dest, "kv_weight": kv_weight, "kv_gain": kv_gain, "cache": cache, "cache_len": cache_len, "step_hidden": step_hidden, "queries": queries}


def normalize(projected, kv_gain):
    latent = projected[..., :LATENT]
    mean_square = lax.optimization_barrier(jnp.mean(latent * latent, axis=-1, keepdims=True))
    scaled = latent * lax.rsqrt(mean_square + 1e-06) * kv_gain
    return jnp.concatenate([scaled, projected[..., LATENT:]], axis=-1).astype(jnp.bfloat16)

def attend(query_block, all_keys, visible):
    score_scale = (NOPE + ROPE) ** (-0.5)
    scores = jnp.einsum('rhc,rjc->rhj', query_block.astype(jnp.float32), all_keys.astype(jnp.float32)) * score_scale
    masked = jnp.where(visible[:, None, :], scores, -jnp.inf)
    top_score = lax.optimization_barrier(jnp.max(masked, axis=-1, keepdims=True))
    expo = jnp.exp(masked - top_score)
    weights = (expo / lax.optimization_barrier(jnp.sum(expo, axis=-1, keepdims=True))).astype(jnp.bfloat16)
    mixed = jnp.einsum('rhj,rjc->rhc', weights.astype(jnp.float32), all_keys[..., :LATENT].astype(jnp.float32))
    return mixed.astype(jnp.bfloat16)

def reference(prompt_hidden, prompt_len, prompt_dest, kv_weight, kv_gain, cache, cache_len, step_hidden, queries):
    prompt_rows = prompt_hidden.reshape(ROWS * PLEN, D)
    projected = jnp.dot(prompt_rows, kv_weight, preferred_element_type=jnp.float32)
    pages = normalize(projected, kv_gain).reshape(ROWS, PLEN, WIDTH)
    step_projected = jnp.dot(step_hidden.reshape(STEPS * ROWS, D), kv_weight, preferred_element_type=jnp.float32)
    fresh = normalize(step_projected, kv_gain).reshape(STEPS, ROWS, WIDTH)
    row_owner = jnp.argsort(prompt_dest).astype(jnp.int32)
    arrived = pages[row_owner]
    arrived_len = prompt_len[row_owner]
    all_keys = jnp.concatenate([cache, arrived, jnp.transpose(fresh, (1, 0, 2))], axis=1)
    position = jnp.arange(CTX + PLEN + STEPS, dtype=jnp.int32)[None, :]
    outputs = []
    for step_index in range(STEPS):
        resident = position < cache_len[:, None]
        prompt_part = (position >= CTX) & (position < CTX + arrived_len[:, None])
        fresh_part = (position >= CTX + PLEN) & (position <= CTX + PLEN + step_index)
        visible = resident | prompt_part | fresh_part
        outputs.append(attend(queries[step_index], all_keys, visible))
    return jnp.stack(outputs)
```

```python
import functools

import jax
import jax.numpy as jnp
from jax import lax
from jax.experimental import pallas as pl
from jax.experimental.pallas import tpu as pltpu
from jax.sharding import PartitionSpec as P

ROPE = 64
NOPE = 128
BLOCKS = 4
TILE = 16
MESH = pl.DeviceIdType.MESH


def ring_place(index, n, snake):
    if not snake:
        return index
    plane, column = lax.div(index, 2), lax.rem(index, 2)
    return plane + column * (n - 1 - 2 * plane)


def ring_index(place, n, snake):
    place = lax.rem(place + n, n)
    if not snake:
        return place
    back = lax.div(place, n // 2)
    return (1 - back) * 2 * place + back * (2 * (n - 1 - place) + 1)


def project_kernel(
    n,
    cap,
    snake,
    send_prompt,
    hidden,
    step_rows,
    weight,
    gain,
    labels,
    inbox,
    meta,
    fresh,
    hbuf,
    wall,
    acc,
    other,
    pages,
    outbox,
    local_sem,
    ring_send,
    ring_recv,
    cross_send,
    cross_recv,
    pair_send,
    pair_recv,
    page_send,
    page_recv,
    mate_send,
    mate_recv,
    meta_send,
    meta_recv,
):
    rows, tokens, depth = hidden.shape
    half = tokens // 2
    shard, width = weight.shape
    latent_width = gain.shape[1]
    near = ((shard + TILE - 1) // (3 * TILE)) * TILE
    far = shard - near
    steps = n // 2

    group = lax.axis_index("groups")
    me = lax.axis_index("seq")
    core = lax.axis_index("head")
    side = lax.rem(group, 2)
    twin = {"groups": group + 1 - 2 * side, "seq": me, "head": core}
    mate = {"groups": group, "seq": me, "head": 1 - core}

    def peer(index):
        return {"groups": group, "seq": index, "head": core}

    place = ring_place(me, n, snake)

    own = pltpu.make_async_copy(weight, wall.at[me], local_sem.at[0])
    own.start()
    loads = [
        pltpu.make_async_copy(
            hidden.at[:, pl.ds(pl.multiple_of((1 - core) * half, half), half), :],
            hbuf.at[pl.ds(0, rows)],
            local_sem.at[1],
        ),
        pltpu.make_async_copy(step_rows, hbuf.at[rows], local_sem.at[2]),
        pltpu.make_async_copy(
            hidden.at[:, pl.ds(pl.multiple_of(core * half, half), half), :],
            hbuf.at[pl.ds(rows + 1, rows)],
            local_sem.at[3],
        ),
    ]

    barrier = pltpu.get_barrier_semaphore()
    for offset in range(1, n):
        pl.semaphore_signal(
            barrier, inc=1, device_id=peer(lax.rem(me + offset, n)), device_id_type=MESH
        )
    pl.semaphore_signal(barrier, inc=1, device_id=twin, device_id_type=MESH)
    pl.semaphore_signal(barrier, inc=1, device_id=mate, device_id_type=MESH)
    pl.semaphore_wait(barrier, n + 1)
    own.wait()

    def span(chunk, which):
        if chunk == 0:
            return pl.ds(pl.multiple_of(which * far, TILE), near)
        return pl.ds(near, far - near)

    def ring_copy(way, step, chunk):
        sign = 1 - 2 * way
        block = wall.at[ring_index(place - sign * (step - 1), n, snake), span(chunk, side)]
        return pltpu.make_async_remote_copy(
            src_ref=block,
            dst_ref=block,
            send_sem=ring_send.at[way, step - 1, chunk],
            recv_sem=ring_recv.at[way, step - 1, chunk],
            device_id=peer(ring_index(place + sign, n, snake)),
            device_id_type=MESH,
        )

    def ring_arrival(way, step, chunk):
        sign = 1 - 2 * way
        block = wall.at[ring_index(place - sign * step, n, snake), span(chunk, side)]
        return pltpu.make_async_remote_copy(
            src_ref=block,
            dst_ref=block,
            send_sem=ring_send.at[way, step - 1, chunk],
            recv_sem=ring_recv.at[way, step - 1, chunk],
            device_id=peer(ring_index(place + sign, n, snake)),
            device_id_type=MESH,
        )

    def cross_copy(way, step, which):
        sign = 1 - 2 * way
        block = wall.at[ring_index(place - sign * step, n, snake), span(0, which)]
        return pltpu.make_async_remote_copy(
            src_ref=block,
            dst_ref=block,
            send_sem=cross_send.at[way, step - 1],
            recv_sem=cross_recv.at[way, step - 1],
            device_id=twin,
            device_id_type=MESH,
        )

    def goes(way, step, chunk):
        return step < steps or (step == steps and way == chunk)

    for chunk in (0, 1):
        for way in (0, 1):
            if goes(way, 1, chunk):
                ring_copy(way, 1, chunk).start()
    for load in loads:
        load.start()

    def meta_copy(target, row):
        return pltpu.make_async_remote_copy(
            src_ref=labels.at[target],
            dst_ref=meta.at[row],
            send_sem=meta_send.at[target],
            recv_sem=meta_recv.at[row],
            device_id=peer(target),
            device_id_type=MESH,
        )

    for offset in range(1, n):
        meta_copy(lax.rem(me + offset, n), me).start()
    own_meta = pltpu.make_async_copy(labels.at[me], meta.at[me], local_sem.at[0])
    own_meta.start()
    for load in loads:
        load.wait()

    depth_block = depth // BLOCKS
    shards_block = n // BLOCKS
    lower = pl.ds(0, rows + 1)
    upper = pl.ds(rows + 1, rows)

    def block_at(turn):
        if not snake:
            return jnp.int32(turn)
        plane = lax.div(me, 2)
        late = lax.div(plane, BLOCKS // 2)
        edge = plane + late * (BLOCKS - 1 - 2 * plane)
        base = (jnp.int32(0), jnp.int32(1), 2 + edge, 3 - edge)[turn]
        return base + late * (BLOCKS - 1 - 2 * base)

    def multiply(turn, part, count):
        block = block_at(turn)
        columns = pl.ds(pl.multiple_of(block * depth_block, 128), depth_block)
        left = hbuf[part, :, columns].reshape(count * half, depth_block)
        right = wall[pl.ds(block * shards_block, shards_block)].reshape(depth_block, width)
        product = jnp.dot(left, right, preferred_element_type=jnp.float32)
        product = product.reshape(count, half, width)
        if turn == 0:
            acc[part] = product
        else:
            acc[part] += product

    ready = {2: (0,), 3: (1, 2), 4: (3,)} if snake else {steps: tuple(range(BLOCKS))}
    crossed = []
    for step in range(1, steps + 1):
        for chunk in (0, 1):
            for way in (0, 1):
                if not goes(way, step, chunk):
                    continue
                ring_arrival(way, step, chunk).wait_recv()
                if step < steps and goes(way, step + 1, chunk):
                    ring_copy(way, step + 1, chunk).start()
                if chunk == 0:
                    cross_copy(way, step, side).start()
                    crossed.append((way, step))
        turns = ready.get(step, ())
        if turns:
            for way, when in crossed:
                cross_copy(way, when, 1 - side).wait_recv()
            crossed = []
        for turn in turns:
            multiply(turn, lower, rows + 1)
            if turn == BLOCKS - 1:
                pair = pltpu.make_async_remote_copy(
                    src_ref=acc.at[lower],
                    dst_ref=other,
                    send_sem=pair_send,
                    recv_sem=pair_recv,
                    device_id=mate,
                    device_id_type=MESH,
                )
                pair.start()
            multiply(turn, upper, rows)
    pair.wait()

    scale = gain[...]

    def norm(value):
        latent = value[:, :latent_width]
        mean_square = jnp.mean(latent * latent, axis=-1, keepdims=True)
        return latent * lax.rsqrt(mean_square + 1e-06) * scale, value[:, latent_width:]

    def norm_page(row, carry):
        value = acc[rows + 1 + row] + other[row]
        head_part, tail_part = norm(value)
        pages[row, :, :latent_width] = head_part.astype(jnp.bfloat16)
        pages[row, :, latent_width:] = tail_part.astype(jnp.bfloat16)
        return carry

    lax.fori_loop(0, rows, norm_page, 0)

    def page_copy(target, row):
        return pltpu.make_async_remote_copy(
            src_ref=outbox.at[target],
            dst_ref=inbox.at[core, row],
            send_sem=page_send.at[target],
            recv_sem=page_recv.at[row],
            device_id=peer(target),
            device_id_type=MESH,
        )

    def mate_copy(row, from_outbox, where):
        return pltpu.make_async_remote_copy(
            src_ref=outbox.at[row] if from_outbox else inbox.at[where, row],
            dst_ref=inbox.at[where, row],
            send_sem=mate_send.at[row],
            recv_sem=mate_recv.at[row],
            device_id=mate,
            device_id_type=MESH,
        )

    for offset in list(range(1, n)) + [0]:
        target = lax.rem(me + offset, n)
        for slot in range(cap):
            outbox[target, pl.ds(slot * half, half), :] = pages[send_prompt[target * cap + slot]]
        if offset:
            page_copy(target, me).start()
    own_meta.wait()
    own_page = pltpu.make_async_copy(outbox.at[me], inbox.at[core, me], local_sem.at[0])
    own_page.start()
    mate_copy(me, True, core).start()

    head_part, tail_part = norm(acc[rows] + other[rows])
    fresh[:, :latent_width] = head_part.astype(jnp.bfloat16).astype(jnp.float32)
    fresh[:, latent_width:] = tail_part.astype(jnp.bfloat16).astype(jnp.float32)

    for step in range(1, steps + 1):
        for chunk in (0, 1):
            for way in (0, 1):
                if goes(way, step, chunk):
                    ring_copy(way, step, chunk).wait_send()
                    if chunk == 0:
                        cross_copy(way, step, side).wait_send()
    for offset in range(1, n):
        source = lax.rem(me + n - offset, n)
        page_copy(source, source).wait_recv()
        mate_copy(source, False, core).start()
    for offset in range(1, n):
        target = lax.rem(me + offset, n)
        page_copy(target, me).wait_send()
        meta_copy(target, me).wait_send()
        meta_copy(target, target).wait_recv()
    own_page.wait()
    for offset in range(n):
        source = lax.rem(me + n - offset, n)
        mate_copy(source, offset == 0, 1 - core).wait_recv()
        mate_copy(source, offset == 0, core).wait_send()


def attend_kernel(
    rows, slot_of, arrived_len, cache_len, query, cache, page, fresh, out, recent
):
    row = pl.program_id(0)
    step_count, _, heads, width = query.shape
    latent_width = out.shape[-1]
    half = page.shape[2]
    tokens = 2 * half
    recent[pl.ds(0, tokens), :] = page[...].reshape(tokens, width)
    spot = lax.broadcasted_iota(jnp.int32, (TILE, width), 0)
    tail = jnp.zeros((TILE, width), jnp.float32)
    for step in range(step_count):
        tail = jnp.where(spot == step, fresh[pl.ds(step * rows + row, 1), :], tail)
    recent[pl.ds(tokens, TILE), :] = tail.astype(jnp.bfloat16)

    score_scale = (NOPE + ROPE) ** (-0.5)
    asked = query[...].reshape(step_count * heads, width)
    resident_keys = cache[0]
    recent_keys = recent[...]
    contract = (((1,), (1,)), ((), ()))
    old = lax.dot_general(asked, resident_keys, contract, preferred_element_type=jnp.float32)
    new = lax.dot_general(asked, recent_keys, contract, preferred_element_type=jnp.float32)
    old_spot = lax.broadcasted_iota(jnp.int32, old.shape, 1)
    new_spot = lax.broadcasted_iota(jnp.int32, new.shape, 1)
    step_of = lax.div(lax.broadcasted_iota(jnp.int32, new.shape, 0), heads)
    old = jnp.where(old_spot < cache_len[row], old * score_scale, -jnp.inf)
    seen = (new_spot < arrived_len[row]) | (
        (new_spot >= tokens) & (new_spot <= tokens + step_of)
    )
    new = jnp.where(seen, new * score_scale, -jnp.inf)
    top = jnp.maximum(
        jnp.max(old, axis=-1, keepdims=True), jnp.max(new, axis=-1, keepdims=True)
    )
    old = jnp.exp(old - top)
    new = jnp.exp(new - top)
    inverse = 1.0 / (
        jnp.sum(old, axis=-1, keepdims=True) + jnp.sum(new, axis=-1, keepdims=True)
    )
    mixed = jnp.dot(
        (old * inverse).astype(jnp.bfloat16),
        resident_keys[:, :latent_width],
        preferred_element_type=jnp.float32,
    ) + jnp.dot(
        (new * inverse).astype(jnp.bfloat16),
        recent_keys[:, :latent_width],
        preferred_element_type=jnp.float32,
    )
    out[...] = mixed.astype(jnp.bfloat16).reshape(out.shape)


def on_device(
    snake,
    prompt_hidden,
    prompt_len,
    prompt_dest,
    kv_weight,
    kv_gain,
    cache,
    cache_len,
    step_hidden,
    queries,
):
    rows, tokens, depth = prompt_hidden.shape
    step_count = step_hidden.shape[0]
    shard, width = kv_weight.shape
    resident_slots = cache.shape[1]
    latent_width = kv_gain.shape[0]
    heads = queries.shape[2]
    n = lax.axis_size("seq")
    cap = max(1, 2 * rows // n)
    half = tokens // 2

    step_rows = step_hidden.reshape(step_count * rows, depth)
    step_rows = jnp.pad(step_rows, ((0, half - step_count * rows), (0, 0)))

    target = prompt_dest // rows
    ids = jnp.arange(rows, dtype=jnp.int32)
    earlier = (ids[None, :] < ids[:, None]) & (target[None, :] == target[:, None])
    send_slot = target * cap + jnp.sum(earlier.astype(jnp.int32), axis=1)
    slots = jnp.arange(n * cap, dtype=jnp.int32)
    fits = send_slot[None, :] == slots[:, None]
    send_prompt = jnp.sum(jnp.where(fits, ids[None, :], 0), axis=1)
    label_row = jnp.sum(jnp.where(fits, prompt_dest[None, :] % rows + 1, 0), axis=1) - 1
    label_len = jnp.sum(jnp.where(fits, prompt_len[None, :], 0), axis=1)
    labels = jnp.stack([label_row.reshape(n, cap), label_len.reshape(n, cap)], axis=1)
    labels = jnp.pad(labels, ((0, 0), (0, 6), (0, 128 - cap)))

    dma = pltpu.SemaphoreType.DMA
    anywhere = pl.BlockSpec(memory_space=pl.ANY)
    in_vmem = pl.BlockSpec(memory_space=pltpu.VMEM)
    inbox, meta, fresh = pl.pallas_call(
        functools.partial(project_kernel, n, cap, snake),
        out_shape=(
            jax.ShapeDtypeStruct((2, n, cap * half, width), jnp.bfloat16),
            jax.ShapeDtypeStruct((n, 8, 128), jnp.int32),
            jax.ShapeDtypeStruct((half, width), jnp.float32),
        ),
        in_specs=[
            pl.BlockSpec(memory_space=pltpu.SMEM),
            anywhere,
            anywhere,
            anywhere,
            in_vmem,
            anywhere,
        ],
        out_specs=(anywhere, anywhere, in_vmem),
        scratch_shapes=[
            pltpu.VMEM((2 * rows + 1, half, depth), jnp.bfloat16),
            pltpu.VMEM((n, shard, width), jnp.bfloat16),
            pltpu.VMEM((2 * rows + 1, half, width), jnp.float32),
            pltpu.VMEM((rows + 1, half, width), jnp.float32),
            pltpu.VMEM((rows, half, width), jnp.bfloat16),
            pltpu.VMEM((n, cap * half, width), jnp.bfloat16),
            dma((4,)),
            dma((2, n // 2, 2)),
            dma((2, n // 2, 2)),
            dma((2, n // 2)),
            dma((2, n // 2)),
            dma,
            dma,
            dma((n,)),
            dma((n,)),
            dma((n,)),
            dma((n,)),
            dma((n,)),
            dma((n,)),
        ],
        compiler_params=pltpu.CompilerParams(
            collective_id=0, has_side_effects=True, vmem_limit_bytes=48 * 1024 * 1024
        ),
    )(
        send_prompt,
        prompt_hidden,
        step_rows,
        kv_weight,
        kv_gain.reshape(1, latent_width),
        labels,
    )

    came_row = meta[:, 0, :cap].reshape(-1)
    came_len = meta[:, 1, :cap].reshape(-1)
    match = came_row[None, :] == ids[:, None]
    slot_of = jnp.sum(jnp.where(match, slots[None, :], 0), axis=1)
    arrived_len = jnp.sum(jnp.where(match, came_len[None, :], 0), axis=1)

    return pl.pallas_call(
        functools.partial(attend_kernel, rows),
        grid_spec=pltpu.PrefetchScalarGridSpec(
            num_scalar_prefetch=3,
            grid=(rows,),
            in_specs=[
                pl.BlockSpec((step_count, 1, heads, width), lambda r, *_: (0, r, 0, 0)),
                pl.BlockSpec((1, resident_slots, width), lambda r, *_: (r, 0, 0)),
                pl.BlockSpec((2, 1, half, width), lambda r, slot, *_: (0, slot[r], 0, 0)),
                pl.BlockSpec((half, width), lambda r, *_: (0, 0)),
            ],
            out_specs=pl.BlockSpec(
                (step_count, 1, heads, latent_width), lambda r, *_: (0, r, 0, 0)
            ),
            scratch_shapes=[pltpu.VMEM((tokens + TILE, width), jnp.bfloat16)],
        ),
        out_shape=jax.ShapeDtypeStruct((step_count, rows, heads, latent_width), jnp.bfloat16),
        compiler_params=pltpu.CompilerParams(vmem_limit_bytes=32 * 1024 * 1024),
    )(
        slot_of,
        arrived_len,
        cache_len,
        queries,
        cache,
        inbox.reshape(2, n * cap, half, width),
        fresh,
    )


def solution(mesh):
    snake = mesh.shape["seq"] == 2 * BLOCKS
    in_specs = (
        P(("groups", "seq"), None, "head"),
        P(("groups", "seq")),
        P(("groups", "seq")),
        P(("head", "seq"), None),
        P(),
        P(("groups", "seq"), None, None),
        P(("groups", "seq")),
        P(None, ("groups", "seq"), "head"),
        P(None, ("groups", "seq"), "head", None),
    )
    out_specs = P(None, ("groups", "seq"), "head", None)
    return jax.shard_map(
        functools.partial(on_device, snake),
        mesh=mesh,
        in_specs=in_specs,
        out_specs=out_specs,
        check_vma=False,
    )
```

```python
import functools

import jax
import jax.numpy as jnp
from jax import lax
from jax.experimental import pallas as pl
from jax.experimental.pallas import tpu as pltpu
from jax.sharding import PartitionSpec as P

ROPE = 64
NOPE = 128
BLOCKS = 4
TILE = 16
MESH = pl.DeviceIdType.MESH


def ring_place(index, n, snake):
    if not snake:
        return index
    plane, column = lax.div(index, 2), lax.rem(index, 2)
    return plane + column * (n - 1 - 2 * plane)


def ring_index(place, n, snake):
    place = lax.rem(place + n, n)
    if not snake:
        return place
    back = lax.div(place, n // 2)
    return (1 - back) * 2 * place + back * (2 * (n - 1 - place) + 1)


def serve_kernel(
    n,
    cap,
    snake,
    prompt_dest,
    prompt_len,
    cache_len,
    hidden,
    step_rows,
    weight,
    gain,
    cache,
    queries,
    out,
    hbuf,
    wall,
    acc,
    other,
    pages,
    outbox,
    inbox,
    labels,
    meta,
    fresh,
    cached,
    asked,
    mixed,
    top,
    total,
    result,
    send_prompt,
    slot_of,
    arrived_len,
    local_sem,
    ring_send,
    ring_recv,
    cross_send,
    cross_recv,
    pair_send,
    pair_recv,
    page_send,
    page_recv,
    mate_send,
    mate_recv,
    meta_send,
    meta_recv,
    out_sem,
):
    rows, tokens, depth = hidden.shape
    half = tokens // 2
    shard, width = weight.shape
    latent_width = gain.shape[1]
    near = ((shard + TILE - 1) // (3 * TILE)) * TILE
    far = shard - near
    steps = n // 2

    group = lax.axis_index("groups")
    me = lax.axis_index("seq")
    core = lax.axis_index("head")
    side = lax.rem(group, 2)
    twin = {"groups": group + 1 - 2 * side, "seq": me, "head": core}
    mate = {"groups": group, "seq": me, "head": 1 - core}

    def peer(index):
        return {"groups": group, "seq": index, "head": core}

    place = ring_place(me, n, snake)

    own = pltpu.make_async_copy(weight, wall.at[me], local_sem.at[0])
    own.start()
    loads = [
        pltpu.make_async_copy(
            hidden.at[:, pl.ds(pl.multiple_of((1 - core) * half, half), half), :],
            hbuf.at[pl.ds(0, rows)],
            local_sem.at[1],
        ),
        pltpu.make_async_copy(step_rows, hbuf.at[rows], local_sem.at[2]),
        pltpu.make_async_copy(
            hidden.at[:, pl.ds(pl.multiple_of(core * half, half), half), :],
            hbuf.at[pl.ds(rows + 1, rows)],
            local_sem.at[3],
        ),
    ]
    late_loads = [
        pltpu.make_async_copy(cache, cached, local_sem.at[4]),
        pltpu.make_async_copy(queries, asked, local_sem.at[5]),
    ]

    barrier = pltpu.get_barrier_semaphore()
    for offset in range(1, n):
        pl.semaphore_signal(
            barrier, inc=1, device_id=peer(lax.rem(me + offset, n)), device_id_type=MESH
        )
    pl.semaphore_signal(barrier, inc=1, device_id=twin, device_id_type=MESH)
    pl.semaphore_signal(barrier, inc=1, device_id=mate, device_id_type=MESH)
    pl.semaphore_wait(barrier, n + 1)
    own.wait()

    def span(chunk, which):
        if chunk == 0:
            return pl.ds(pl.multiple_of(which * far, TILE), near)
        return pl.ds(near, far - near)

    def ring_copy(way, step, chunk):
        sign = 1 - 2 * way
        block = wall.at[ring_index(place - sign * (step - 1), n, snake), span(chunk, side)]
        return pltpu.make_async_remote_copy(
            src_ref=block,
            dst_ref=block,
            send_sem=ring_send.at[way, step - 1, chunk],
            recv_sem=ring_recv.at[way, step - 1, chunk],
            device_id=peer(ring_index(place + sign, n, snake)),
            device_id_type=MESH,
        )

    def ring_arrival(way, step, chunk):
        sign = 1 - 2 * way
        block = wall.at[ring_index(place - sign * step, n, snake), span(chunk, side)]
        return pltpu.make_async_remote_copy(
            src_ref=block,
            dst_ref=block,
            send_sem=ring_send.at[way, step - 1, chunk],
            recv_sem=ring_recv.at[way, step - 1, chunk],
            device_id=peer(ring_index(place + sign, n, snake)),
            device_id_type=MESH,
        )

    def cross_copy(way, step, which):
        sign = 1 - 2 * way
        block = wall.at[ring_index(place - sign * step, n, snake), span(0, which)]
        return pltpu.make_async_remote_copy(
            src_ref=block,
            dst_ref=block,
            send_sem=cross_send.at[way, step - 1],
            recv_sem=cross_recv.at[way, step - 1],
            device_id=twin,
            device_id_type=MESH,
        )

    def goes(way, step, chunk):
        return step < steps or (step == steps and way == chunk)

    for chunk in (0, 1):
        for way in (0, 1):
            if goes(way, 1, chunk):
                ring_copy(way, 1, chunk).start()
    for load in loads:
        load.start()

    for load in late_loads:
        load.start()

    def meta_copy(target, row):
        return pltpu.make_async_remote_copy(
            src_ref=labels,
            dst_ref=meta.at[row],
            send_sem=meta_send.at[target],
            recv_sem=meta_recv.at[row],
            device_id=peer(target),
            device_id_type=MESH,
        )

    lane = lax.broadcasted_iota(jnp.int32, (1, 128), 1)
    dest = jnp.full((1, 128), -1, jnp.int32)
    live = jnp.zeros((1, 128), jnp.int32)
    order = jnp.zeros((1, 128), jnp.int32)
    for prompt in range(rows):
        dest = jnp.where(lane == prompt, prompt_dest[prompt], dest)
        live = jnp.where(lane == prompt, prompt_len[prompt], live)
    owner = jnp.full((1, 128), -1, jnp.int32)
    for prompt in range(rows):
        one = lax.div(prompt_dest[prompt], rows)
        owner = jnp.where(lane == prompt, one, owner)
    for prompt in range(rows):
        one = lax.div(prompt_dest[prompt], rows)
        order = order + jnp.where((lane > prompt) & (owner == one), 1, 0)
    labels[...] = jnp.zeros(labels.shape, jnp.int32)
    labels[0:1, :] = dest
    labels[1:2, :] = live
    labels[2:3, :] = order
    for offset in range(1, n):
        meta_copy(lax.rem(me + offset, n), me).start()
    meta[me] = labels[...]
    place_sent = owner * cap + order

    def find_prompt(slot, carry):
        send_prompt[slot] = jnp.minimum(
            jnp.sum(jnp.where(place_sent == slot, lane, 0)), rows - 1
        )
        return carry

    lax.fori_loop(0, n * cap, find_prompt, 0)
    for load in loads:
        load.wait()

    depth_block = depth // BLOCKS
    shards_block = n // BLOCKS
    lower = pl.ds(0, rows + 1)
    upper = pl.ds(rows + 1, rows)

    def block_at(turn):
        if not snake:
            return jnp.int32(turn)
        plane = lax.div(me, 2)
        late = lax.div(plane, BLOCKS // 2)
        edge = plane + late * (BLOCKS - 1 - 2 * plane)
        base = (jnp.int32(0), jnp.int32(1), 2 + edge, 3 - edge)[turn]
        return base + late * (BLOCKS - 1 - 2 * base)

    def multiply(turn, part, count):
        block = block_at(turn)
        columns = pl.ds(pl.multiple_of(block * depth_block, 128), depth_block)
        left = hbuf[part, :, columns].reshape(count * half, depth_block)
        right = wall[pl.ds(block * shards_block, shards_block)].reshape(depth_block, width)
        product = jnp.dot(left, right, preferred_element_type=jnp.float32)
        product = product.reshape(count, half, width)
        if turn == 0:
            acc[part] = product
        else:
            acc[part] += product

    if snake:
        ready = {(2, 1): (0,), (3, 1): (1,), (4, 0): (2,), (4, 1): (3,)}
    else:
        ready = {(steps, 1): tuple(range(BLOCKS))}
    crossed = []
    for step in range(1, steps + 1):
        for chunk in (0, 1):
            for way in (0, 1):
                if not goes(way, step, chunk):
                    continue
                ring_arrival(way, step, chunk).wait_recv()
                if step < steps and goes(way, step + 1, chunk):
                    ring_copy(way, step + 1, chunk).start()
                if chunk == 0:
                    cross_copy(way, step, side).start()
                    crossed.append((way, step))
            turns = ready.get((step, chunk), ())
            if turns:
                waiting = [pair for pair in crossed if chunk == 1 or pair[1] < step]
                for way, when in waiting:
                    cross_copy(way, when, 1 - side).wait_recv()
                crossed = [pair for pair in crossed if pair not in waiting]
            for turn in turns:
                multiply(turn, lower, rows + 1)
                if turn == BLOCKS - 1:
                    pair = pltpu.make_async_remote_copy(
                        src_ref=acc.at[lower],
                        dst_ref=other,
                        send_sem=pair_send,
                        recv_sem=pair_recv,
                        device_id=mate,
                        device_id_type=MESH,
                    )
                    pair.start()
                multiply(turn, upper, rows)
    pair.wait()

    scale = gain[...]

    def norm(value):
        latent = value[:, :latent_width]
        mean_square = jnp.mean(latent * latent, axis=-1, keepdims=True)
        return latent * lax.rsqrt(mean_square + 1e-06) * scale, value[:, latent_width:]

    def norm_page(row, carry):
        value = acc[rows + 1 + row] + other[row]
        head_part, tail_part = norm(value)
        pages[row, :, :latent_width] = head_part.astype(jnp.bfloat16)
        pages[row, :, latent_width:] = tail_part.astype(jnp.bfloat16)
        return carry

    lax.fori_loop(0, rows, norm_page, 0)

    def page_copy(target, row):
        return pltpu.make_async_remote_copy(
            src_ref=outbox.at[target],
            dst_ref=inbox.at[core, pl.ds(row * cap, cap)],
            send_sem=page_send.at[target],
            recv_sem=page_recv.at[row],
            device_id=peer(target),
            device_id_type=MESH,
        )

    def mate_copy(row, where):
        block = inbox.at[where, pl.ds(row * cap, cap)]
        return pltpu.make_async_remote_copy(
            src_ref=block,
            dst_ref=block,
            send_sem=mate_send.at[row],
            recv_sem=mate_recv.at[row],
            device_id=mate,
            device_id_type=MESH,
        )

    for offset in range(1, n):
        target = lax.rem(me + offset, n)
        for slot in range(cap):
            outbox[target, slot] = pages[send_prompt[target * cap + slot]]
        page_copy(target, me).start()
    for slot in range(cap):
        inbox[core, me * cap + slot] = pages[send_prompt[me * cap + slot]]
    mate_copy(me, core).start()

    head_part, tail_part = norm(acc[rows] + other[rows])
    fresh[:, :latent_width] = head_part.astype(jnp.bfloat16).astype(jnp.float32)
    fresh[:, latent_width:] = tail_part.astype(jnp.bfloat16).astype(jnp.float32)

    for step in range(1, steps + 1):
        for chunk in (0, 1):
            for way in (0, 1):
                if goes(way, step, chunk):
                    ring_copy(way, step, chunk).wait_send()
                    if chunk == 0:
                        cross_copy(way, step, side).wait_send()
    for offset in range(1, n):
        target = lax.rem(me + offset, n)
        meta_copy(target, me).wait_send()
        meta_copy(target, target).wait_recv()
    came = meta[:, 0, :]
    came_len = meta[:, 1, :]
    came_slot = lax.broadcasted_iota(jnp.int32, came.shape, 0) * cap + meta[:, 2, :]

    def find_slot(row, carry):
        here = came == me * rows + row
        slot_of[row] = jnp.minimum(jnp.sum(jnp.where(here, came_slot, 0)), n * cap - 1)
        arrived_len[row] = jnp.sum(jnp.where(here, came_len, 0))
        return carry

    lax.fori_loop(0, rows, find_slot, 0)
    for load in late_loads:
        load.wait()

    step_count, _, heads, _ = queries.shape
    asking = step_count * heads
    score_scale = (NOPE + ROPE) ** (-0.5)
    contract = (((1,), (1,)), ((), ()))

    def against(left, right):
        return lax.dot_general(left, right, contract, preferred_element_type=jnp.float32)

    def attend_resident(row, carry):
        spot = lax.broadcasted_iota(jnp.int32, (TILE, width), 0)
        tail = jnp.zeros((TILE, width), jnp.float32)
        for step in range(step_count):
            tail = jnp.where(spot == step, fresh[pl.ds(step * rows + row, 1), :], tail)
        tail = tail.astype(jnp.bfloat16)
        query = asked[:, row].reshape(asking, width)
        old = jnp.dot(query, cached[row], preferred_element_type=jnp.float32)
        new = against(query, tail)
        old_spot = lax.broadcasted_iota(jnp.int32, old.shape, 1)
        new_spot = lax.broadcasted_iota(jnp.int32, new.shape, 1)
        step_of = lax.div(lax.broadcasted_iota(jnp.int32, new.shape, 0), heads)
        old = jnp.where(old_spot < cache_len[row], old * score_scale, -jnp.inf)
        new = jnp.where(new_spot <= step_of, new * score_scale, -jnp.inf)
        peak = jnp.maximum(
            jnp.max(old, axis=-1, keepdims=True), jnp.max(new, axis=-1, keepdims=True)
        )
        old = jnp.exp(old - peak)
        new = jnp.exp(new - peak)
        top[row] = peak
        total[row] = jnp.sum(old, axis=-1, keepdims=True) + jnp.sum(
            new, axis=-1, keepdims=True
        )
        mixed[row] = against(
            old.astype(jnp.bfloat16), cached[row, pl.ds(0, latent_width), :]
        ) + jnp.dot(
            new.astype(jnp.bfloat16),
            tail[:, :latent_width],
            preferred_element_type=jnp.float32,
        )
        return carry

    done = 0
    for offset in range(1, n):
        until = rows * offset // (n - 1)
        if until > done:
            lax.fori_loop(done, until, attend_resident, 0)
            done = until
        source = lax.rem(me + n - offset, n)
        page_copy(source, source).wait_recv()
        mate_copy(source, core).start()
    for offset in range(1, n):
        page_copy(lax.rem(me + offset, n), me).wait_send()
    for offset in range(n):
        source = lax.rem(me + n - offset, n)
        mate_copy(source, 1 - core).wait_recv()
        mate_copy(source, core).wait_send()

    def out_copy(row):
        return pltpu.make_async_copy(result.at[row], out.at[:, row], out_sem.at[row])

    def attend_prompt(row, carry):
        keys = inbox[:, slot_of[row]].reshape(tokens, width)
        query = asked[:, row].reshape(asking, width)
        score = against(query, keys)
        spot = lax.broadcasted_iota(jnp.int32, score.shape, 1)
        score = jnp.where(spot < arrived_len[row], score * score_scale, -jnp.inf)
        before = top[row]
        peak = jnp.maximum(before, jnp.max(score, axis=-1, keepdims=True))
        fade = jnp.exp(before - peak)
        part = jnp.exp(score - peak)
        inverse = 1.0 / (total[row] * fade + jnp.sum(part, axis=-1, keepdims=True))
        value = mixed[row] * (fade * inverse) + inverse * jnp.dot(
            part.astype(jnp.bfloat16),
            keys[:, :latent_width],
            preferred_element_type=jnp.float32,
        )
        result[row] = value.astype(jnp.bfloat16).reshape(step_count, heads, latent_width)
        out_copy(row).start()
        return carry

    lax.fori_loop(0, rows, attend_prompt, 0, unroll=2)
    for row in range(rows):
        out_copy(row).wait()


def on_device(
    snake,
    prompt_hidden,
    prompt_len,
    prompt_dest,
    kv_weight,
    kv_gain,
    cache,
    cache_len,
    step_hidden,
    queries,
):
    rows, tokens, depth = prompt_hidden.shape
    step_count = step_hidden.shape[0]
    shard, width = kv_weight.shape
    resident_slots = cache.shape[1]
    latent_width = kv_gain.shape[0]
    heads = queries.shape[2]
    n = lax.axis_size("seq")
    cap = max(1, 2 * rows // n)
    half = tokens // 2

    step_rows = step_hidden.reshape(step_count * rows, depth)
    step_rows = jnp.pad(step_rows, ((0, half - step_count * rows), (0, 0)))

    dma = pltpu.SemaphoreType.DMA
    anywhere = pl.BlockSpec(memory_space=pl.ANY)
    scalars = pl.BlockSpec(memory_space=pltpu.SMEM)
    asking = step_count * heads
    return pl.pallas_call(
        functools.partial(serve_kernel, n, cap, snake),
        out_shape=jax.ShapeDtypeStruct((step_count, rows, heads, latent_width), jnp.bfloat16),
        in_specs=[scalars] * 3
        + [anywhere] * 3
        + [pl.BlockSpec(memory_space=pltpu.VMEM)]
        + [anywhere] * 2,
        out_specs=anywhere,
        scratch_shapes=[
            pltpu.VMEM((2 * rows + 1, half, depth), jnp.bfloat16),
            pltpu.VMEM((n, shard, width), jnp.bfloat16),
            pltpu.VMEM((2 * rows + 1, half, width), jnp.float32),
            pltpu.VMEM((rows + 1, half, width), jnp.float32),
            pltpu.VMEM((rows, half, width), jnp.bfloat16),
            pltpu.VMEM((n, cap, half, width), jnp.bfloat16),
            pltpu.VMEM((2, n * cap, half, width), jnp.bfloat16),
            pltpu.VMEM((8, 128), jnp.int32),
            pltpu.VMEM((n, 8, 128), jnp.int32),
            pltpu.VMEM((half, width), jnp.float32),
            pltpu.VMEM((rows, width, resident_slots), jnp.bfloat16),
            pltpu.VMEM(queries.shape, jnp.bfloat16),
            pltpu.VMEM((rows, asking, latent_width), jnp.float32),
            pltpu.VMEM((rows, asking, 1), jnp.float32),
            pltpu.VMEM((rows, asking, 1), jnp.float32),
            pltpu.VMEM((rows, step_count, heads, latent_width), jnp.bfloat16),
            pltpu.SMEM((n * cap,), jnp.int32),
            pltpu.SMEM((rows,), jnp.int32),
            pltpu.SMEM((rows,), jnp.int32),
            dma((6,)),
            dma((2, n // 2, 2)),
            dma((2, n // 2, 2)),
            dma((2, n // 2)),
            dma((2, n // 2)),
            dma,
            dma,
            dma((n,)),
            dma((n,)),
            dma((n,)),
            dma((n,)),
            dma((n,)),
            dma((n,)),
            dma((rows,)),
        ],
        compiler_params=pltpu.CompilerParams(
            collective_id=0, has_side_effects=True, vmem_limit_bytes=60 * 1024 * 1024
        ),
    )(
        prompt_dest,
        prompt_len,
        cache_len,
        prompt_hidden,
        step_rows,
        kv_weight,
        kv_gain.reshape(1, latent_width),
        jnp.transpose(cache, (0, 2, 1)),
        queries,
    )


def solution(mesh):
    snake = mesh.shape["seq"] == 2 * BLOCKS
    in_specs = (
        P(("groups", "seq"), None, "head"),
        P(("groups", "seq")),
        P(("groups", "seq")),
        P(("head", "seq"), None),
        P(),
        P(("groups", "seq"), None, None),
        P(("groups", "seq")),
        P(None, ("groups", "seq"), "head"),
        P(None, ("groups", "seq"), "head", None),
    )
    out_specs = P(None, ("groups", "seq"), "head", None)
    return jax.shard_map(
        functools.partial(on_device, snake),
        mesh=mesh,
        in_specs=in_specs,
        out_specs=out_specs,
        check_vma=False,
    )
```

```python
import functools

import jax
import jax.numpy as jnp
from jax import lax
from jax.experimental import pallas as pl
from jax.experimental.pallas import tpu as pltpu
from jax.sharding import PartitionSpec as P

ROPE = 64
NOPE = 128
BLOCKS = 4
TILE = 16
MESH = pl.DeviceIdType.MESH


def ring_place(index, n, snake):
    if not snake:
        return index
    plane, column = lax.div(index, 2), lax.rem(index, 2)
    return plane + column * (n - 1 - 2 * plane)


def ring_index(place, n, snake):
    place = lax.rem(place + n, n)
    if not snake:
        return place
    back = lax.div(place, n // 2)
    return (1 - back) * 2 * place + back * (2 * (n - 1 - place) + 1)


def serve_kernel(
    n,
    cap,
    snake,
    prompt_dest,
    prompt_len,
    cache_len,
    hidden,
    step_rows,
    weight,
    gain,
    cache,
    queries,
    out,
    hbuf,
    wall,
    acc,
    sent,
    other,
    pages,
    outbox,
    inbox,
    labels,
    meta,
    fresh,
    cached,
    asked,
    mixed,
    top,
    total,
    result,
    send_prompt,
    slot_of,
    arrived_len,
    local_sem,
    ring_send,
    ring_recv,
    cross_send,
    cross_recv,
    pair_send,
    pair_recv,
    page_send,
    page_recv,
    mate_send,
    mate_recv,
    meta_send,
    meta_recv,
    out_sem,
):
    rows, tokens, depth = hidden.shape
    half = tokens // 2
    shard, width = weight.shape
    latent_width = gain.shape[1]
    near = ((shard + TILE - 1) // (3 * TILE)) * TILE
    far = shard - near
    steps = n // 2

    group = lax.axis_index("groups")
    me = lax.axis_index("seq")
    core = lax.axis_index("head")
    side = lax.rem(group, 2)
    twin = {"groups": group + 1 - 2 * side, "seq": me, "head": core}
    mate = {"groups": group, "seq": me, "head": 1 - core}

    def peer(index):
        return {"groups": group, "seq": index, "head": core}

    place = ring_place(me, n, snake)

    own = pltpu.make_async_copy(weight, wall.at[me], local_sem.at[0])
    own.start()
    loads = [
        pltpu.make_async_copy(
            hidden.at[:, pl.ds(pl.multiple_of((1 - core) * half, half), half), :],
            hbuf.at[pl.ds(0, rows)],
            local_sem.at[1],
        ),
        pltpu.make_async_copy(
            hidden.at[:, pl.ds(pl.multiple_of(core * half, half), half), :],
            hbuf.at[pl.ds(rows + 1, rows)],
            local_sem.at[3],
        ),
    ]
    late_loads = [
        pltpu.make_async_copy(cache, cached, local_sem.at[4]),
        pltpu.make_async_copy(queries, asked, local_sem.at[5]),
    ]

    barrier = pltpu.get_barrier_semaphore()
    for offset in range(1, n):
        pl.semaphore_signal(
            barrier, inc=1, device_id=peer(lax.rem(me + offset, n)), device_id_type=MESH
        )
    pl.semaphore_signal(barrier, inc=1, device_id=twin, device_id_type=MESH)
    pl.semaphore_signal(barrier, inc=1, device_id=mate, device_id_type=MESH)
    pl.semaphore_wait(barrier, n + 1)
    own.wait()

    def span(chunk, which):
        if chunk == 0:
            return pl.ds(pl.multiple_of(which * far, TILE), near)
        return pl.ds(near, far - near)

    def ring_copy(way, step, chunk):
        sign = 1 - 2 * way
        block = wall.at[ring_index(place - sign * (step - 1), n, snake), span(chunk, side)]
        return pltpu.make_async_remote_copy(
            src_ref=block,
            dst_ref=block,
            send_sem=ring_send.at[way, step - 1, chunk],
            recv_sem=ring_recv.at[way, step - 1, chunk],
            device_id=peer(ring_index(place + sign, n, snake)),
            device_id_type=MESH,
        )

    def ring_arrival(way, step, chunk):
        sign = 1 - 2 * way
        block = wall.at[ring_index(place - sign * step, n, snake), span(chunk, side)]
        return pltpu.make_async_remote_copy(
            src_ref=block,
            dst_ref=block,
            send_sem=ring_send.at[way, step - 1, chunk],
            recv_sem=ring_recv.at[way, step - 1, chunk],
            device_id=peer(ring_index(place + sign, n, snake)),
            device_id_type=MESH,
        )

    def cross_copy(way, step, which):
        sign = 1 - 2 * way
        block = wall.at[ring_index(place - sign * step, n, snake), span(0, which)]
        return pltpu.make_async_remote_copy(
            src_ref=block,
            dst_ref=block,
            send_sem=cross_send.at[way, step - 1],
            recv_sem=cross_recv.at[way, step - 1],
            device_id=twin,
            device_id_type=MESH,
        )

    def goes(way, step, chunk):
        return step < steps or (step == steps and way == chunk)

    for chunk in (0, 1):
        for way in (0, 1):
            if goes(way, 1, chunk):
                ring_copy(way, 1, chunk).start()
    for load in loads:
        load.start()
    spare = jnp.zeros((half - step_rows.shape[0], depth), jnp.bfloat16)
    hbuf[rows] = jnp.concatenate([step_rows[...], spare], axis=0)

    for load in late_loads:
        load.start()

    def meta_copy(target, row):
        return pltpu.make_async_remote_copy(
            src_ref=labels,
            dst_ref=meta.at[row],
            send_sem=meta_send.at[target],
            recv_sem=meta_recv.at[row],
            device_id=peer(target),
            device_id_type=MESH,
        )

    lane = lax.broadcasted_iota(jnp.int32, (1, 128), 1)
    dest = jnp.full((1, 128), -1, jnp.int32)
    live = jnp.zeros((1, 128), jnp.int32)
    order = jnp.zeros((1, 128), jnp.int32)
    for prompt in range(rows):
        dest = jnp.where(lane == prompt, prompt_dest[prompt], dest)
        live = jnp.where(lane == prompt, prompt_len[prompt], live)
    owner = jnp.full((1, 128), -1, jnp.int32)
    for prompt in range(rows):
        one = lax.div(prompt_dest[prompt], rows)
        owner = jnp.where(lane == prompt, one, owner)
    for prompt in range(rows):
        one = lax.div(prompt_dest[prompt], rows)
        order = order + jnp.where((lane > prompt) & (owner == one), 1, 0)
    labels[...] = jnp.zeros(labels.shape, jnp.int32)
    labels[0:1, :] = dest
    labels[1:2, :] = live
    labels[2:3, :] = order
    for offset in range(1, n):
        meta_copy(lax.rem(me + offset, n), me).start()
    meta[me] = labels[...]
    place_sent = owner * cap + order

    def find_prompt(slot, carry):
        send_prompt[slot] = jnp.minimum(
            jnp.sum(jnp.where(place_sent == slot, lane, 0)), rows - 1
        )
        return carry

    lax.fori_loop(0, n * cap, find_prompt, 0, unroll=8)
    for load in loads:
        load.wait()

    depth_block = depth // BLOCKS
    shards_block = n // BLOCKS
    lower = pl.ds(0, rows + 1)
    upper = pl.ds(rows + 1, rows)

    def block_at(turn):
        if not snake:
            return jnp.int32(turn)
        plane = lax.div(me, 2)
        late = lax.div(plane, BLOCKS // 2)
        edge = plane + late * (BLOCKS - 1 - 2 * plane)
        base = (jnp.int32(0), jnp.int32(1), 2 + edge, 3 - edge)[turn]
        return base + late * (BLOCKS - 1 - 2 * base)

    def multiply(turn, part, count):
        block = block_at(turn)
        columns = pl.ds(pl.multiple_of(block * depth_block, 128), depth_block)
        left = hbuf[part, :, columns].reshape(count * half, depth_block)
        right = wall[pl.ds(block * shards_block, shards_block)].reshape(depth_block, width)
        product = jnp.dot(left, right, preferred_element_type=jnp.float32)
        product = product.reshape(count, half, width)
        if turn == 0:
            acc[part] = product
        elif turn == BLOCKS - 1 and count > rows:
            whole = acc[part] + product
            sent[...] = whole.astype(jnp.bfloat16)
            acc[rows] = whole[rows]
        else:
            acc[part] += product

    if snake:
        ready = {(2, 1): (0,), (3, 1): (1,), (4, 0): (2,), (4, 1): (3,)}
    else:
        ready = {(steps, 1): tuple(range(BLOCKS))}
    crossed = []
    for step in range(1, steps + 1):
        for chunk in (0, 1):
            for way in (0, 1):
                if not goes(way, step, chunk):
                    continue
                ring_arrival(way, step, chunk).wait_recv()
                if step < steps and goes(way, step + 1, chunk):
                    ring_copy(way, step + 1, chunk).start()
                if chunk == 0:
                    cross_copy(way, step, side).start()
                    crossed.append((way, step))
            turns = ready.get((step, chunk), ())
            if turns:
                waiting = [pair for pair in crossed if chunk == 1 or pair[1] < step]
                for way, when in waiting:
                    cross_copy(way, when, 1 - side).wait_recv()
                crossed = [pair for pair in crossed if pair not in waiting]
            for turn in turns:
                multiply(turn, lower, rows + 1)
                if turn == BLOCKS - 1:
                    pair = pltpu.make_async_remote_copy(
                        src_ref=sent,
                        dst_ref=other,
                        send_sem=pair_send,
                        recv_sem=pair_recv,
                        device_id=mate,
                        device_id_type=MESH,
                    )
                    pair.start()
                multiply(turn, upper, rows)
    pair.wait()

    scale = gain[...]

    def norm(value):
        latent = value[:, :latent_width]
        mean_square = jnp.mean(latent * latent, axis=-1, keepdims=True)
        return latent * lax.rsqrt(mean_square + 1e-06) * scale, value[:, latent_width:]

    def norm_page(row, carry):
        value = acc[rows + 1 + row] + other[row].astype(jnp.float32)
        head_part, tail_part = norm(value)
        pages[row, :, :latent_width] = head_part.astype(jnp.bfloat16)
        pages[row, :, latent_width:] = tail_part.astype(jnp.bfloat16)
        return carry

    lax.fori_loop(0, rows, norm_page, 0, unroll=2)

    def page_copy(target, row):
        return pltpu.make_async_remote_copy(
            src_ref=outbox.at[target],
            dst_ref=inbox.at[core, pl.ds(row * cap, cap)],
            send_sem=page_send.at[target],
            recv_sem=page_recv.at[row],
            device_id=peer(target),
            device_id_type=MESH,
        )

    def mate_copy(row, where):
        block = inbox.at[where, pl.ds(row * cap, cap)]
        return pltpu.make_async_remote_copy(
            src_ref=block,
            dst_ref=block,
            send_sem=mate_send.at[row],
            recv_sem=mate_recv.at[row],
            device_id=mate,
            device_id_type=MESH,
        )

    for offset in range(1, n):
        target = lax.rem(me + offset, n)
        for slot in range(cap):
            outbox[target, slot] = pages[send_prompt[target * cap + slot]]
        page_copy(target, me).start()
    for slot in range(cap):
        inbox[core, me * cap + slot] = pages[send_prompt[me * cap + slot]]
    mate_copy(me, core).start()

    head_part, tail_part = norm(acc[rows] + other[rows].astype(jnp.float32))
    fresh[:, :latent_width] = head_part.astype(jnp.bfloat16).astype(jnp.float32)
    fresh[:, latent_width:] = tail_part.astype(jnp.bfloat16).astype(jnp.float32)

    for step in range(1, steps + 1):
        for chunk in (0, 1):
            for way in (0, 1):
                if goes(way, step, chunk):
                    ring_copy(way, step, chunk).wait_send()
                    if chunk == 0:
                        cross_copy(way, step, side).wait_send()
    for offset in range(1, n):
        target = lax.rem(me + offset, n)
        meta_copy(target, me).wait_send()
        meta_copy(target, target).wait_recv()
    came = meta[:, 0, :]
    came_len = meta[:, 1, :]
    came_slot = lax.broadcasted_iota(jnp.int32, came.shape, 0) * cap + meta[:, 2, :]

    def find_slot(row, carry):
        here = came == me * rows + row
        slot_of[row] = jnp.minimum(jnp.sum(jnp.where(here, came_slot, 0)), n * cap - 1)
        arrived_len[row] = jnp.sum(jnp.where(here, came_len, 0))
        return carry

    lax.fori_loop(0, rows, find_slot, 0, unroll=6)
    for load in late_loads:
        load.wait()

    step_count, _, heads, _ = queries.shape
    asking = step_count * heads
    score_scale = (NOPE + ROPE) ** (-0.5)
    contract = (((1,), (1,)), ((), ()))

    def against(left, right):
        return lax.dot_general(left, right, contract, preferred_element_type=jnp.float32)

    def attend_resident(row, carry):
        spot = lax.broadcasted_iota(jnp.int32, (TILE, width), 0)
        tail = jnp.zeros((TILE, width), jnp.float32)
        for step in range(step_count):
            tail = jnp.where(spot == step, fresh[pl.ds(step * rows + row, 1), :], tail)
        tail = tail.astype(jnp.bfloat16)
        query = asked[:, row].reshape(asking, width)
        old = jnp.dot(query, cached[row], preferred_element_type=jnp.float32)
        new = against(query, tail)
        old_spot = lax.broadcasted_iota(jnp.int32, old.shape, 1)
        new_spot = lax.broadcasted_iota(jnp.int32, new.shape, 1)
        step_of = lax.div(lax.broadcasted_iota(jnp.int32, new.shape, 0), heads)
        old = jnp.where(old_spot < cache_len[row], old * score_scale, -jnp.inf)
        new = jnp.where(new_spot <= step_of, new * score_scale, -jnp.inf)
        peak = jnp.maximum(
            jnp.max(old, axis=-1, keepdims=True), jnp.max(new, axis=-1, keepdims=True)
        )
        old = jnp.exp(old - peak)
        new = jnp.exp(new - peak)
        top[row] = peak
        total[row] = jnp.sum(old, axis=-1, keepdims=True) + jnp.sum(
            new, axis=-1, keepdims=True
        )
        mixed[row] = against(
            old.astype(jnp.bfloat16), cached[row, pl.ds(0, latent_width), :]
        ) + jnp.dot(
            new.astype(jnp.bfloat16),
            tail[:, :latent_width],
            preferred_element_type=jnp.float32,
        )
        return carry

    done = 0
    for offset in range(1, n):
        until = rows * offset // (n - 1)
        if until > done:
            lax.fori_loop(done, until, attend_resident, 0)
            done = until
        source = lax.rem(me + n - offset, n)
        page_copy(source, source).wait_recv()
        mate_copy(source, core).start()
    for offset in range(1, n):
        page_copy(lax.rem(me + offset, n), me).wait_send()
    for offset in range(n):
        source = lax.rem(me + n - offset, n)
        mate_copy(source, 1 - core).wait_recv()
        mate_copy(source, core).wait_send()

    def out_copy(row):
        return pltpu.make_async_copy(result.at[row], out.at[:, row], out_sem.at[row])

    def attend_prompt(row, carry):
        keys = inbox[:, slot_of[row]].reshape(tokens, width)
        query = asked[:, row].reshape(asking, width)
        score = against(query, keys)
        spot = lax.broadcasted_iota(jnp.int32, score.shape, 1)
        score = jnp.where(spot < arrived_len[row], score * score_scale, -jnp.inf)
        before = top[row]
        peak = jnp.maximum(before, jnp.max(score, axis=-1, keepdims=True))
        fade = jnp.exp(before - peak)
        part = jnp.exp(score - peak)
        inverse = 1.0 / (total[row] * fade + jnp.sum(part, axis=-1, keepdims=True))
        value = mixed[row] * (fade * inverse) + inverse * jnp.dot(
            part.astype(jnp.bfloat16),
            keys[:, :latent_width],
            preferred_element_type=jnp.float32,
        )
        result[row] = value.astype(jnp.bfloat16).reshape(step_count, heads, latent_width)
        out_copy(row).start()
        return carry

    lax.fori_loop(0, rows, attend_prompt, 0, unroll=4)
    for row in range(rows):
        out_copy(row).wait()


def on_device(
    snake,
    prompt_hidden,
    prompt_len,
    prompt_dest,
    kv_weight,
    kv_gain,
    cache,
    cache_len,
    step_hidden,
    queries,
):
    rows, tokens, depth = prompt_hidden.shape
    step_count = step_hidden.shape[0]
    shard, width = kv_weight.shape
    resident_slots = cache.shape[1]
    latent_width = kv_gain.shape[0]
    heads = queries.shape[2]
    n = lax.axis_size("seq")
    cap = max(1, 2 * rows // n)
    half = tokens // 2

    step_rows = step_hidden.reshape(step_count * rows, depth)

    dma = pltpu.SemaphoreType.DMA
    anywhere = pl.BlockSpec(memory_space=pl.ANY)
    in_hbm = pl.BlockSpec(memory_space=pltpu.HBM)
    in_vmem = pl.BlockSpec(memory_space=pltpu.VMEM)
    scalars = pl.BlockSpec(memory_space=pltpu.SMEM)
    asking = step_count * heads
    return pl.pallas_call(
        functools.partial(serve_kernel, n, cap, snake),
        out_shape=jax.ShapeDtypeStruct((step_count, rows, heads, latent_width), jnp.bfloat16),
        in_specs=[scalars] * 3
        + [in_hbm, in_vmem, in_hbm, in_vmem, in_hbm, in_hbm],
        out_specs=anywhere,
        scratch_shapes=[
            pltpu.VMEM((2 * rows + 1, half, depth), jnp.bfloat16),
            pltpu.VMEM((n, shard, width), jnp.bfloat16),
            pltpu.VMEM((2 * rows + 1, half, width), jnp.float32),
            pltpu.VMEM((rows + 1, half, width), jnp.bfloat16),
            pltpu.VMEM((rows + 1, half, width), jnp.bfloat16),
            pltpu.VMEM((rows, half, width), jnp.bfloat16),
            pltpu.VMEM((n, cap, half, width), jnp.bfloat16),
            pltpu.VMEM((2, n * cap, half, width), jnp.bfloat16),
            pltpu.VMEM((8, 128), jnp.int32),
            pltpu.VMEM((n, 8, 128), jnp.int32),
            pltpu.VMEM((half, width), jnp.float32),
            pltpu.VMEM((rows, width, resident_slots), jnp.bfloat16),
            pltpu.VMEM(queries.shape, jnp.bfloat16),
            pltpu.VMEM((rows, asking, latent_width), jnp.float32),
            pltpu.VMEM((rows, asking, 1), jnp.float32),
            pltpu.VMEM((rows, asking, 1), jnp.float32),
            pltpu.VMEM((rows, step_count, heads, latent_width), jnp.bfloat16),
            pltpu.SMEM((n * cap,), jnp.int32),
            pltpu.SMEM((rows,), jnp.int32),
            pltpu.SMEM((rows,), jnp.int32),
            dma((6,)),
            dma((2, n // 2, 2)),
            dma((2, n // 2, 2)),
            dma((2, n // 2)),
            dma((2, n // 2)),
            dma,
            dma,
            dma((n,)),
            dma((n,)),
            dma((n,)),
            dma((n,)),
            dma((n,)),
            dma((n,)),
            dma((rows,)),
        ],
        compiler_params=pltpu.CompilerParams(
            collective_id=0, has_side_effects=True, vmem_limit_bytes=60300 * 1024
        ),
    )(
        prompt_dest,
        prompt_len,
        cache_len,
        prompt_hidden,
        step_rows,
        kv_weight,
        kv_gain.reshape(1, latent_width),
        jnp.transpose(cache, (0, 2, 1)),
        queries,
    )


def solution(mesh):
    snake = mesh.shape["seq"] == 2 * BLOCKS
    in_specs = (
        P(("groups", "seq"), None, "head"),
        P(("groups", "seq")),
        P(("groups", "seq")),
        P(("head", "seq"), None),
        P(),
        P(("groups", "seq"), None, None),
        P(("groups", "seq")),
        P(None, ("groups", "seq"), "head"),
        P(None, ("groups", "seq"), "head", None),
    )
    out_specs = P(None, ("groups", "seq"), "head", None)
    return jax.shard_map(
        functools.partial(on_device, snake),
        mesh=mesh,
        in_specs=in_specs,
        out_specs=out_specs,
        check_vma=False,
    )
```
